32 devices in a mesh: groups: 2 (over y), dom: 4 (over x, core), sub: 4 (over z).
Axes of the slice: x: 2, y: 2, z: 4, core: 2. Of those that a mesh axis runs over, the one named last changes fastest.
Arguments:
- orbitals: float32 [64, 131072], P(None, ('groups', 'dom', 'sub')), parts along dimension 1, may hold values from -6 to 6
- mass_inv: float32 [131072], P(('groups', 'dom', 'sub')), parts along dimension 0, may hold values from 0.5 to 2
- potential: float32 [131072], P(('groups', 'dom', 'sub')), parts along dimension 0, may hold values from -1 to 1
- elem_scale: float32 [4096], P(('groups', 'dom', 'sub')), parts along dimension 0, may hold values from 0.3 to 3
- connectivity: int32 [125, 4096], P(None, ('groups', 'dom', 'sub')), parts along dimension 1, may hold values from 0 to 5631, as said below
- elem_count: int32 [32], P(('groups', 'dom', 'sub')), parts along dimension 0, may hold values from 64 to 128, as said below
- owner_node: int32 [32, 3, 4, 128], P(('groups', 'dom', 'sub')), parts along dimension 0, may hold values from 0 to 4096, as said below
- elem_matrix: float32 [125, 125], replicated
Outputs:
- filtered_one: float32 [64, 131072], P(None, ('groups', 'dom', 'sub')), parts along dimension 1
- filtered_two: float32 [64, 131072], P(None, ('groups', 'dom', 'sub')), parts along dimension 1
The draws below stay inside these ranges and needn't reach their ends.
There are 2 independent parts, one for each index of `groups`. The reference program is written for one: setup_inputs(seed, part) draws one part's arguments, and reference() takes and returns one part's arrays. A program takes and returns all parts, laid end to end along the dimension named above; an argument that names none is the same for every part. Nothing has to cross between parts.
Inputs may be any that keep to these rules, and one draw needn't show every extreme that they name: `elem_count`: some device has exactly 128 elements. `connectivity`: an entry below 4096 names an owned node; an entry 4096 or more names a ghost slot that some owner lists in owner_node. `owner_node`: for each owner, plane q and peer sub index c, the used slots are k below a count of at most 128, the rest hold 4096; some plane of some device uses all 128 slots. Slots toward oneself, toward the plane below dom index 0 and above dom index 3 are unused.
All inputs are finite; a program needn't handle non-finite values.
Results may differ from the reference program's by a relative error of at most 0.0003.
Values sent between devices are 32-bit elements; how exact they have to be, the bound alone decides.
A program may use at most 128 MiB of HBM per device.

```python
import math
import jax
import jax.numpy as jnp
from jax import lax

ORB = 64
NODES_EL = 125
OWN = 4096
E_MAX = 128
CAP = 128
NODES = 65536
ELEMS = 2048
N_DOM = 4
N_SUB = 4


def interface_tables(key):
    key = jax.random.fold_in(key, 11)
    key_count, key_dom, key_sub, key_nodes = jax.random.split(key, 4)
    counts = jax.random.randint(key_count, (N_DOM, N_SUB, 3, N_SUB), CAP // 4, CAP + 1)
    dom_pos = jnp.arange(N_DOM)[:, None, None, None]
    sub_pos = jnp.arange(N_SUB)[None, :, None, None]
    plane = jnp.arange(3)[None, None, :, None]
    target = jnp.arange(N_SUB)[None, None, None, :]
    full_dom = jax.random.randint(key_dom, (), 0, N_DOM)
    full_sub = jax.random.randint(key_sub, (), 0, N_SUB)
    forced = (dom_pos == full_dom) & (sub_pos == full_sub) & (plane == 1) & (target == (full_sub + 1) % N_SUB)
    counts = jnp.where(forced, CAP, counts)
    usable = jnp.logical_not((plane == 1) & (target == sub_pos))
    usable = usable & jnp.logical_not((plane == 0) & (dom_pos == 0))
    usable = usable & jnp.logical_not((plane == 2) & (dom_pos == N_DOM - 1))
    counts = jnp.where(usable, counts, 0)
    live = jnp.arange(CAP)[None, None, None, None, :] < counts[..., None]
    nodes = jax.random.randint(key_nodes, (N_DOM, N_SUB, 3, N_SUB, CAP), 0, OWN)
    return (live, nodes)


def draw_owner_node(key, part):
    live, nodes = interface_tables(key)
    marked = jnp.where(live, nodes, OWN)
    padded = jnp.pad(marked, ((1, 1), (0, 0), (0, 0), (0, 0), (0, 0)), constant_values=OWN)
    planes = [padded[plane:plane + N_DOM, :, 2 - plane].transpose(0, 2, 1, 3) for plane in range(3)]
    return jnp.stack(planes, 2).reshape(N_DOM * N_SUB, 3, N_SUB, CAP).astype(jnp.int32)


def draw_connectivity(key, part):
    live, nodes = interface_tables(key)
    key = jax.random.fold_in(key, 5)
    dev_total = N_DOM * N_SUB
    ghost_total = 3 * N_SUB * CAP
    picks = jax.random.randint(key, (dev_total, NODES_EL * E_MAX), 0, OWN + ghost_total)
    live_flat = live.reshape(dev_total, ghost_total)
    ghost_pos = jnp.clip(picks - OWN, 0, ghost_total - 1)
    alive = jnp.take_along_axis(live_flat, ghost_pos, axis=1)
    chosen = jnp.where((picks < OWN) | alive, picks, picks % OWN)
    chosen = chosen.reshape(dev_total, NODES_EL, E_MAX).transpose(1, 0, 2)
    return chosen.reshape(NODES_EL, dev_total * E_MAX).astype(jnp.int32)


def draw_elem_count(key, part):
    key = jax.random.fold_in(key, 7)
    key_count, key_full = jax.random.split(key)
    dev_total = N_DOM * N_SUB
    counts = jax.random.randint(key_count, (dev_total,), E_MAX // 2, E_MAX + 1)
    full_dev = jax.random.randint(key_full, (), 0, dev_total)
    return jnp.where(jnp.arange(dev_total) == full_dev, E_MAX, counts).astype(jnp.int32)


def draw_elem_matrix(key, part):
    key = jax.random.fold_in(key, 9)
    key_off, key_diag = jax.random.split(key)
    noise = jax.random.normal(key_off, (NODES_EL, NODES_EL), jnp.float32)
    diag_vals = jax.random.uniform(key_diag, (NODES_EL,), jnp.float32, 1.0, 2.0)
    return (0.03 * (noise + noise.T) + jnp.eye(NODES_EL, dtype=jnp.float32) * diag_vals).astype(jnp.float32)


def shard_levels(own_key, shape, cuts, low, high):
    gain = 1.0
    for dim, shards_of in cuts:
        heights = jax.random.uniform(jax.random.fold_in(jax.random.fold_in(own_key, 6), dim), (shards_of,), jnp.float32, low / len(cuts), high / len(cuts))
        gain = gain * jnp.repeat(jnp.exp(heights), shape[dim] // shards_of).reshape((-1,) + (1,) * (len(shape) - 1 - dim))
    return gain


def centred(key, dims, spread, limit, shards=(), held_as=jnp.bfloat16):
    result = spread * jax.random.normal(key, dims, jnp.float32)
    if shards:
        result = result * shard_levels(key, dims, shards, -0.22, 0.18)
    return jnp.clip(result, -limit, limit).astype(held_as)


def setup_inputs(seed: int = 0, part: int = 0) -> dict:
    key_list = jax.random.split(jax.random.key(seed), 9)
    part_splits = jax.random.split(jax.random.fold_in(key_list[8], part), 9)
    orbitals = centred(part_splits[0], (ORB, NODES), 1.0, 6.0, ((1, 16),), jnp.float32)
    mass_inv = jnp.clip(jnp.exp(math.log(2.0) - 1.3862944 * jax.random.uniform(part_splits[1], (NODES,), jnp.float32) ** shard_levels(part_splits[1], (NODES,), ((0, 16),), -0.2, 0.2)), 0.5, 2.0)
    potential = jnp.clip(jax.random.uniform(part_splits[2], (NODES,), jnp.float32, -1.0, 1.0) * shard_levels(part_splits[2], (NODES,), ((0, 16),), -0.4, 0.0), -1.0, 1.0)
    elem_scale = jnp.clip(jnp.exp(math.log(3.0) - 2.3025851 * jax.random.uniform(part_splits[3], (ELEMS,), jnp.float32) ** shard_levels(part_splits[3], (ELEMS,), ((0, 16),), -0.2, 0.2)), 0.3, 3.0)
    connectivity = draw_connectivity(jax.random.fold_in(jax.random.fold_in(key_list[8], part), 71), part)
    elem_count = draw_elem_count(jax.random.fold_in(jax.random.fold_in(key_list[8], part), 71), part)
    owner_node = draw_owner_node(jax.random.fold_in(jax.random.fold_in(key_list[8], part), 71), part)
    elem_matrix = draw_elem_matrix(jax.random.fold_in(key_list[8], 71), part)
    return {"orbitals": orbitals, "mass_inv": mass_inv, "potential": potential, "elem_scale": elem_scale, "connectivity": connectivity, "elem_count": elem_count, "owner_node": owner_node, "elem_matrix": elem_matrix}


shift_center = 0.5
first_gain = 0.8
second_gain = 1.2
memory_gain = 0.5


def reference(orbitals, mass_inv, potential, elem_scale, connectivity, elem_count, owner_node, elem_matrix):
    dev_total = N_DOM * N_SUB
    orb_rows = orbitals.shape[0]
    ghost_total = 3 * N_SUB * CAP
    start_field = orbitals.reshape(orb_rows, dev_total, OWN).transpose(1, 0, 2)
    mass_dev = mass_inv.reshape(dev_total, 1, OWN)
    pot_dev = potential.reshape(dev_total, 1, OWN)
    conn_dev = connectivity.reshape(NODES_EL, dev_total, E_MAX).transpose(1, 0, 2)
    scale_dev = elem_scale.reshape(dev_total, E_MAX)
    receive = owner_node.reshape(dev_total, ghost_total)

    def route(buffer):
        grid = buffer.reshape(N_DOM, N_SUB, orb_rows, 3, N_SUB, CAP)
        grid = jnp.pad(grid, ((1, 1), (0, 0), (0, 0), (0, 0), (0, 0), (0, 0)))
        planes = [grid[plane:plane + N_DOM, :, :, 2 - plane].transpose(0, 3, 2, 1, 4) for plane in range(3)]
        return jnp.stack(planes, 3).reshape(dev_total, orb_rows, ghost_total)

    def take_cols(values, index):
        return jnp.take(values, index, axis=1)

    def add_cols(values, index, extra):
        return values.at[:, index].add(extra)

    def fetch(field):
        padded = jnp.concatenate([field, jnp.zeros((dev_total, orb_rows, 1), field.dtype)], axis=2)
        outgoing = jax.vmap(take_cols)(padded, receive)
        return route(outgoing)

    def local(inputs):
        node_table, columns, scales, elem_total = inputs
        weight = jnp.where(jnp.arange(E_MAX, dtype=jnp.int32) < elem_total, scales, jnp.zeros_like(scales))
        flat = columns.reshape(-1)
        gathered = jnp.take(node_table, flat, axis=1).reshape(orb_rows, NODES_EL, E_MAX) * weight
        terms = jnp.einsum("ab,obe->oae", elem_matrix, gathered, precision=lax.Precision.HIGHEST)
        totals = jnp.zeros(node_table.shape, node_table.dtype)
        return totals.at[:, flat].add(terms.reshape(orb_rows, -1))

    def apply_ham(field):
        node_table = jnp.concatenate([field, fetch(field)], axis=2)
        sums = lax.map(local, (node_table, conn_dev, scale_dev, elem_count))
        arrived = route(sums[:, :, OWN:])
        owned_pad = jnp.concatenate([sums[:, :, :OWN], jnp.zeros((dev_total, orb_rows, 1), field.dtype)], axis=2)
        owned_pad = jax.vmap(add_cols)(owned_pad, receive, arrived)
        return mass_dev * 0.5 * owned_pad[:, :, :OWN] + pot_dev * field

    first = first_gain * (apply_ham(start_field) - shift_center * start_field)
    second = second_gain * (apply_ham(first) - shift_center * first) - memory_gain * start_field
    return (first.transpose(1, 0, 2).reshape(orb_rows, dev_total * OWN),
            second.transpose(1, 0, 2).reshape(orb_rows, dev_total * OWN))
```

```python
import functools

import jax
import jax.numpy as jnp
from jax import lax
from jax.experimental import pallas as pl
from jax.experimental.pallas import tpu as pltpu
from jax.sharding import PartitionSpec as P

shift_center = 0.5
first_gain = 0.8
second_gain = 1.2
memory_gain = 0.5

LANES = 128
MESH = pl.DeviceIdType.MESH
VMEM_LIMIT = 58 * 1024 * 1024
BANKS = 8


def vmem():
    return pl.BlockSpec(memory_space=pltpu.VMEM)


def smem():
    return pl.BlockSpec(memory_space=pltpu.SMEM)


def low_half(shape):
    return lax.broadcasted_iota(jnp.int32, shape, len(shape) - 1) < LANES // 2


def pack_rows(owner_s, table, packed):
    blocks, half = packed.shape[0], packed.shape[1]
    mask = low_half((1, LANES))

    @pl.loop(0, blocks)
    def _(block):
        for k in range(half):
            low = table[pl.ds(owner_s[block, k], 1), :]
            high = table[pl.ds(owner_s[block, half + k], 1), :]
            packed[block, pl.ds(k, 1), :] = jnp.where(mask, low, high)


def start_kernel(owner_s, field, table, packed):
    nodes = field.shape[1]
    for at in range(0, nodes, LANES):
        piece = field[:, at : at + LANES]
        table[at : at + LANES, :] = jnp.concatenate([piece, piece], axis=0).T
    table[nodes:, :] = jnp.zeros((table.shape[0] - nodes, LANES), jnp.float32)
    pack_rows(owner_s, table, packed)


def exchange_kernel(doms, subs, send, recv, send_sem, recv_sem):
    grp = lax.axis_index("groups")
    dom = lax.axis_index("dom")
    sub = lax.axis_index("sub")
    barrier = pltpu.get_barrier_semaphore()

    def each(action):
        for plane in range(3):
            for peer in range(subs):
                there = dom + plane - 1
                live = jnp.logical_and(there >= 0, there < doms)
                if plane == 1:
                    live = jnp.logical_and(live, sub != peer)

                @pl.when(live)
                def _():
                    action(plane, peer, there)

    def greet(plane, peer, there):
        pl.semaphore_signal(
            barrier, inc=1, device_id=(grp, there, peer), device_id_type=MESH
        )

    def copy(plane, peer, there):
        return pltpu.make_async_remote_copy(
            src_ref=send.at[plane * subs + peer],
            dst_ref=recv.at[(2 - plane) * subs + sub],
            send_sem=send_sem.at[plane * subs + peer],
            recv_sem=recv_sem.at[(2 - plane) * subs + sub],
            device_id=(grp, there, peer),
            device_id_type=MESH,
        )

    def arrival(plane, peer, there):
        return pltpu.make_async_remote_copy(
            src_ref=send.at[plane * subs + peer],
            dst_ref=recv.at[plane * subs + peer],
            send_sem=send_sem.at[plane * subs + peer],
            recv_sem=recv_sem.at[plane * subs + peer],
            device_id=(grp, there, peer),
            device_id_type=MESH,
        )

    each(greet)
    planes = jnp.where(dom > 0, 2, 1) + jnp.where(dom < doms - 1, 1, 0)
    pl.semaphore_wait(barrier, planes * subs - 1)
    each(lambda *where: copy(*where).start())
    each(lambda *where: copy(*where).wait_send())
    each(lambda *where: arrival(*where).wait_recv())


def element_kernel(conn_s, table, ghosts, matrix, weight, owned, partial, full, mat, work, *banks):
    nodes = owned.shape[0]
    blocks, half = ghosts.shape[0], ghosts.shape[1]
    rows = matrix.shape[0]
    pairs = conn_s.shape[1] // 2
    mask = low_half((1, LANES))

    mat[...] = jnp.zeros_like(mat)
    mat[:rows, : matrix.shape[1]] = matrix[...]
    full[:nodes, :] = table[:nodes, :]
    for block in range(blocks):
        piece = ghosts[block]
        other = pltpu.roll(piece, LANES // 2, axis=1)
        begin = nodes + block * 2 * half
        wide = low_half(piece.shape)
        full[begin : begin + half, :] = jnp.where(wide, piece, other)
        full[begin + half : begin + 2 * half, :] = jnp.where(wide, other, piece)
    tail = rows - rows % 8
    work[:, tail:, :] = jnp.zeros((pairs, work.shape[1] - tail, LANES), jnp.float32)

    @pl.loop(0, rows)
    def _(j):
        for pair in range(pairs):
            low = full[pl.ds(conn_s[j, 2 * pair], 1), :]
            high = full[pl.ds(conn_s[j, 2 * pair + 1], 1), :]
            work[pair, pl.ds(j, 1), :] = jnp.where(mask, low, high)

    big = mat[...].astype(jnp.bfloat16)
    small = (mat[...] - big.astype(jnp.float32)).astype(jnp.bfloat16)
    step = 4

    @pl.loop(0, pairs // step)
    def _(n):
        piece = jnp.concatenate(
            [work[n * step + k] * weight[n * step + k] for k in range(step)], axis=1
        )
        high = piece.astype(jnp.bfloat16)
        low = (piece - high.astype(jnp.float32)).astype(jnp.bfloat16)
        dot = functools.partial(jnp.dot, preferred_element_type=jnp.float32)
        piece = dot(big, high) + (dot(big, low) + dot(small, high))
        for k in range(step):
            work[n * step + k] = piece[:, k * LANES : (k + 1) * LANES]

    zero = jnp.zeros((8, LANES), jnp.float32)

    @pl.loop(0, full.shape[0] // 64)
    def _(n):
        for bank in banks:
            for r in range(8):
                bank[pl.ds(pl.multiple_of(n * 64 + r * 8, 8), 8), :] = zero

    @pl.loop(0, rows)
    def _(i):
        for pair in range(pairs):
            term = work[pair, pl.ds(i, 1), :]
            for side in range(2):
                bank = banks[(2 * pair + side) % len(banks)]
                at = pl.ds(conn_s[i, 2 * pair + side], 1)
                bank[at, :] = bank[at, :] + term

    def summed(begin, size):
        at = pl.ds(begin, size)
        low = sum([bank[at, :] for bank in banks[2::2]], banks[0][at, :])
        high = sum([bank[at, :] for bank in banks[3::2]], banks[1][at, :])
        both = low_half((size, LANES))
        total = jnp.where(both, low, high)
        return total + pltpu.roll(total, LANES // 2, axis=1)

    @pl.loop(0, nodes // 128)
    def _(n):
        begin = pl.multiple_of(n * 128, 128)
        owned[pl.ds(begin, 128), :] = summed(begin, 128)

    @pl.loop(0, blocks)
    def _(block):
        begin = pl.multiple_of(nodes + block * 2 * half, 64)
        partial[block] = jnp.where(
            low_half((half, LANES)), summed(begin, half), summed(begin + half, half)
        )


def collect(owner_s, arrived, owned, banks):
    nodes = owned.shape[0]
    blocks, half = arrived.shape[0], arrived.shape[1]
    banks[0][:nodes, :] = owned[...]
    for bank in banks[1:]:
        bank[...] = jnp.zeros_like(bank)

    @pl.loop(0, blocks)
    def _(block):
        for k in range(half):
            term = arrived[block, pl.ds(k, 1), :]
            for side in range(2):
                bank = banks[(2 * k + side) % len(banks)]
                at = pl.ds(owner_s[block, side * half + k], 1)
                bank[at, :] = bank[at, :] + term


def assembled_columns(banks, at):
    rows = pl.ds(at, LANES)
    low = sum([bank[rows, :] for bank in banks[2::2]], banks[0][rows, :])
    high = sum([bank[rows, :] for bank in banks[3::2]], banks[1][rows, :])
    both = jnp.where(low_half((LANES, LANES)), low, high).T
    return both[: LANES // 2] + both[LANES // 2 :]


def first_kernel(owner_s, arrived, owned, field, mass, pot, first, table, packed, *banks):
    nodes = field.shape[1]
    collect(owner_s, arrived, owned, banks)
    for at in range(0, nodes, LANES):
        cols = slice(at, at + LANES)
        v = field[:, cols]
        ham = mass[:, cols] * 0.5 * assembled_columns(banks, at) + pot[:, cols] * v
        piece = first_gain * (ham - shift_center * v)
        first[:, cols] = piece
        table[cols, :] = jnp.concatenate([piece, piece], axis=0).T
    table[nodes:, :] = jnp.zeros((table.shape[0] - nodes, LANES), jnp.float32)
    pack_rows(owner_s, table, packed)


def second_kernel(owner_s, arrived, owned, field, older, mass, pot, second, *banks):
    nodes = field.shape[1]
    collect(owner_s, arrived, owned, banks)
    for at in range(0, nodes, LANES):
        cols = slice(at, at + LANES)
        v = field[:, cols]
        ham = mass[:, cols] * 0.5 * assembled_columns(banks, at) + pot[:, cols] * v
        second[:, cols] = second_gain * (ham - shift_center * v) - memory_gain * older[:, cols]


def on_device(
    orbitals, mass_inv, potential, elem_scale, connectivity, elem_count, owner_node, elem_matrix
):
    orbs, nodes = orbitals.shape
    doms = lax.axis_size("dom")
    subs = lax.axis_size("sub")
    cap = owner_node.shape[3]
    elems = elem_scale.shape[0]
    blocks, half = 3 * subs, cap // 2
    rows_up = (elem_matrix.shape[0] + 127) // 128 * 128
    f32 = jnp.float32
    params = pltpu.CompilerParams(vmem_limit_bytes=VMEM_LIMIT)

    owner = owner_node.reshape(blocks, cap)
    mass = mass_inv.reshape(1, nodes)
    pot = potential.reshape(1, nodes)
    weight = jnp.where(jnp.arange(elems, dtype=jnp.int32) < elem_count[0], elem_scale, 0.0)
    weight = jnp.repeat(weight, orbs).reshape(elems // 2, 1, LANES)

    table_shape = jax.ShapeDtypeStruct((nodes + 8, LANES), f32)
    block_shape = jax.ShapeDtypeStruct((blocks, half, LANES), f32)
    field_shape = jax.ShapeDtypeStruct((orbs, nodes), f32)
    owned_shape = jax.ShapeDtypeStruct((nodes, LANES), f32)

    exchange = pl.pallas_call(
        functools.partial(exchange_kernel, doms, subs),
        out_shape=block_shape,
        in_specs=[vmem()],
        out_specs=vmem(),
        scratch_shapes=[
            pltpu.SemaphoreType.DMA((blocks,)),
            pltpu.SemaphoreType.DMA((blocks,)),
        ],
        compiler_params=pltpu.CompilerParams(
            collective_id=0, has_side_effects=True, vmem_limit_bytes=VMEM_LIMIT
        ),
        name="exchange",
    )
    total = nodes + blocks * cap
    element = pl.pallas_call(
        element_kernel,
        out_shape=(owned_shape, block_shape),
        in_specs=[smem(), vmem(), vmem(), vmem(), vmem()],
        out_specs=(vmem(), vmem()),
        scratch_shapes=[
            pltpu.VMEM((total, LANES), f32),
            pltpu.VMEM((rows_up, rows_up), f32),
            pltpu.VMEM((elems // 2, rows_up, LANES), f32),
        ]
        + [pltpu.VMEM((total, LANES), f32)] * BANKS,
        compiler_params=params,
        name="element",
    )
    owner_banks = [pltpu.VMEM((nodes + 8, LANES), f32)] * 4

    table, packed = pl.pallas_call(
        start_kernel,
        out_shape=(table_shape, block_shape),
        in_specs=[smem(), vmem()],
        out_specs=(vmem(), vmem()),
        compiler_params=params,
        name="start",
    )(owner, orbitals)
    owned, partial = element(connectivity, table, exchange(packed), elem_matrix, weight)
    first, table, packed = pl.pallas_call(
        first_kernel,
        out_shape=(field_shape, table_shape, block_shape),
        in_specs=[smem()] + [vmem()] * 5,
        out_specs=(vmem(),) * 3,
        scratch_shapes=owner_banks,
        compiler_params=params,
        name="first",
    )(owner, exchange(partial), owned, orbitals, mass, pot)
    owned, partial = element(connectivity, table, exchange(packed), elem_matrix, weight)
    second = pl.pallas_call(
        second_kernel,
        out_shape=field_shape,
        in_specs=[smem()] + [vmem()] * 6,
        out_specs=vmem(),
        scratch_shapes=owner_banks,
        compiler_params=params,
        name="second",
    )(owner, exchange(partial), owned, first, orbitals, mass, pot)
    return (first, second)


def solution(mesh):
    placed = (
        P(None, ("groups", "dom", "sub")),
        P(("groups", "dom", "sub")),
        P(("groups", "dom", "sub")),
        P(("groups", "dom", "sub")),
        P(None, ("groups", "dom", "sub")),
        P(("groups", "dom", "sub")),
        P(("groups", "dom", "sub"), None, None, None),
        P(),
    )
    return jax.shard_map(
        on_device,
        mesh=mesh,
        in_specs=placed,
        out_specs=(P(None, ("groups", "dom", "sub")), P(None, ("groups", "dom", "sub"))),
        check_vma=False,
    )
```

```python
import functools

import jax
import jax.numpy as jnp
from jax import lax
from jax.experimental import pallas as pl
from jax.experimental.pallas import tpu as pltpu
from jax.sharding import PartitionSpec as P

shift_center = 0.5
first_gain = 0.8
second_gain = 1.2
memory_gain = 0.5

LANES = 128
MESH = pl.DeviceIdType.MESH
VMEM_LIMIT = 58 * 1024 * 1024
BANKS = 8


def vmem():
    return pl.BlockSpec(memory_space=pltpu.VMEM)


def smem():
    return pl.BlockSpec(memory_space=pltpu.SMEM)


def low_half(shape):
    return lax.broadcasted_iota(jnp.int32, shape, len(shape) - 1) < LANES // 2


def slot(owner_s, block, k):
    subs = owner_s.shape[2]
    return owner_s[0, block // subs, block % subs, k]


def pack_rows(owner_s, table, packed):
    blocks, half = packed.shape[0], packed.shape[1]
    mask = low_half((1, LANES))

    @pl.loop(0, blocks)
    def _(block):
        for k in range(half):
            low = table[pl.ds(slot(owner_s, block, k), 1), :]
            high = table[pl.ds(slot(owner_s, block, half + k), 1), :]
            packed[block, pl.ds(k, 1), :] = jnp.where(mask, low, high)


def start_kernel(owner_s, field, table, packed):
    nodes = field.shape[1]
    for at in range(0, nodes, LANES):
        piece = field[:, at : at + LANES]
        table[at : at + LANES, :] = jnp.concatenate([piece, piece], axis=0).T
    table[nodes:, :] = jnp.zeros((table.shape[0] - nodes, LANES), jnp.float32)
    pack_rows(owner_s, table, packed)


def exchange_kernel(doms, subs, send, recv, send_sem, recv_sem):
    grp = lax.axis_index("groups")
    dom = lax.axis_index("dom")
    sub = lax.axis_index("sub")
    barrier = pltpu.get_barrier_semaphore()

    def each(action):
        for plane in range(3):
            for peer in range(subs):
                there = dom + plane - 1
                live = jnp.logical_and(there >= 0, there < doms)
                if plane == 1:
                    live = jnp.logical_and(live, sub != peer)

                @pl.when(live)
                def _():
                    action(plane, peer, there)

    def greet(plane, peer, there):
        pl.semaphore_signal(
            barrier, inc=1, device_id=(grp, there, peer), device_id_type=MESH
        )

    def copy(plane, peer, there):
        return pltpu.make_async_remote_copy(
            src_ref=send.at[plane * subs + peer],
            dst_ref=recv.at[(2 - plane) * subs + sub],
            send_sem=send_sem.at[plane * subs + peer],
            recv_sem=recv_sem.at[(2 - plane) * subs + sub],
            device_id=(grp, there, peer),
            device_id_type=MESH,
        )

    def arrival(plane, peer, there):
        return pltpu.make_async_remote_copy(
            src_ref=send.at[plane * subs + peer],
            dst_ref=recv.at[plane * subs + peer],
            send_sem=send_sem.at[plane * subs + peer],
            recv_sem=recv_sem.at[plane * subs + peer],
            device_id=(grp, there, peer),
            device_id_type=MESH,
        )

    each(greet)
    planes = jnp.where(dom > 0, 2, 1) + jnp.where(dom < doms - 1, 1, 0)
    pl.semaphore_wait(barrier, planes * subs - 1)
    each(lambda *where: copy(*where).start())
    each(lambda *where: copy(*where).wait_send())
    each(lambda *where: arrival(*where).wait_recv())


def element_kernel(
    conn, scale_s, count_s, table, ghosts, matrix, owned, partial, full, mat, work, copied, *scratch
):
    nodes = owned.shape[0]
    blocks, half = ghosts.shape[0], ghosts.shape[1]
    rows = matrix.shape[0]
    pairs = work.shape[0]
    groups = -(-rows // 8)
    conn_s, banks = scratch[:groups], scratch[groups:]
    mask = low_half((1, LANES))

    copies = []
    for group in range(groups):
        size = min(8, rows - 8 * group)
        copies.append(
            pltpu.make_async_copy(
                conn.at[pl.ds(8 * group, size)],
                conn_s[group].at[pl.ds(0, size)],
                copied.at[group],
            )
        )
        copies[-1].start()

    mat[...] = jnp.zeros_like(mat)
    mat[:rows, : matrix.shape[1]] = matrix[...]
    full[:nodes, :] = table[:nodes, :]
    for block in range(blocks):
        piece = ghosts[block]
        other = pltpu.roll(piece, LANES // 2, axis=1)
        begin = nodes + block * 2 * half
        wide = low_half(piece.shape)
        full[begin : begin + half, :] = jnp.where(wide, piece, other)
        full[begin + half : begin + 2 * half, :] = jnp.where(wide, other, piece)
    tail = rows - rows % 8
    work[:, tail:, :] = jnp.zeros((pairs, work.shape[1] - tail, LANES), jnp.float32)
    for copy in copies:
        copy.wait()

    zero = jnp.zeros((8, LANES), jnp.float32)
    share = full.shape[0] // pairs

    @pl.loop(0, pairs)
    def _(pair):
        for j in range(rows):
            low = full[pl.ds(conn_s[j // 8][j % 8, pair], 1), :]
            high = full[pl.ds(conn_s[j // 8][j % 8, pairs + pair], 1), :]
            work[pair, j : j + 1, :] = jnp.where(mask, low, high)
        for bank in banks:
            for r in range(0, share, 8):
                bank[pl.ds(pl.multiple_of(pair * share + r, 8), 8), :] = zero

    big = mat[...].astype(jnp.bfloat16)
    small = (mat[...] - big.astype(jnp.float32)).astype(jnp.bfloat16)
    step = 4

    def weight(pair):
        low = jnp.where(pair < count_s[0], scale_s[pair], 0.0)
        high = jnp.where(pairs + pair < count_s[0], scale_s[pairs + pair], 0.0)
        return jnp.where(mask, low, high)

    @pl.loop(0, pairs // step)
    def _(n):
        piece = jnp.concatenate(
            [work[n * step + k] * weight(n * step + k) for k in range(step)], axis=1
        )
        high = piece.astype(jnp.bfloat16)
        low = (piece - high.astype(jnp.float32)).astype(jnp.bfloat16)
        dot = functools.partial(jnp.dot, preferred_element_type=jnp.float32)
        piece = dot(big, high) + (dot(big, low) + dot(small, high))
        for k in range(step):
            work[n * step + k] = piece[:, k * LANES : (k + 1) * LANES]

    @pl.loop(0, pairs)
    def _(pair):
        for i in range(rows):
            term = work[pair, i : i + 1, :]
            for side in range(2):
                bank = banks[(2 * i + side) % len(banks)]
                at = pl.ds(conn_s[i // 8][i % 8, side * pairs + pair], 1)
                bank[at, :] = bank[at, :] + term

    def summed(begin, size):
        at = pl.ds(begin, size)
        low = sum([bank[at, :] for bank in banks[2::2]], banks[0][at, :])
        high = sum([bank[at, :] for bank in banks[3::2]], banks[1][at, :])
        return jnp.where(low_half((size, LANES)), low, high)

    def doubled(begin, size):
        total = summed(begin, size)
        return total + pltpu.roll(total, LANES // 2, axis=1)

    @pl.loop(0, nodes // 64)
    def _(n):
        begin = pl.multiple_of(n * 64, 64)
        owned[pl.ds(begin, 64), :] = summed(begin, 64)

    @pl.loop(0, blocks)
    def _(block):
        begin = pl.multiple_of(nodes + block * 2 * half, 64)
        partial[block] = jnp.where(
            low_half((half, LANES)), doubled(begin, half), doubled(begin + half, half)
        )


def collect(owner_s, arrived, owned, banks):
    nodes = owned.shape[0]
    blocks, half = arrived.shape[0], arrived.shape[1]
    for bank in banks[:2]:
        bank[:nodes, :] = owned[...]
    for bank in banks[2:]:
        bank[...] = jnp.zeros_like(bank)

    @pl.loop(0, blocks)
    def _(block):
        for k in range(half):
            term = arrived[block, pl.ds(k, 1), :]
            for side in range(2):
                bank = banks[(2 * k + side) % len(banks)]
                at = pl.ds(slot(owner_s, block, side * half + k), 1)
                bank[at, :] = bank[at, :] + term


def assembled_columns(banks, at):
    rows = pl.ds(at, LANES)
    low = sum([bank[rows, :] for bank in banks[2::2]], banks[0][rows, :])
    high = sum([bank[rows, :] for bank in banks[3::2]], banks[1][rows, :])
    both = jnp.where(low_half((LANES, LANES)), low, high).T
    return both[: LANES // 2] + both[LANES // 2 :]


def first_kernel(owner_s, arrived, owned, field, mass, pot, first, table, packed, *banks):
    nodes = field.shape[1]
    collect(owner_s, arrived, owned, banks)
    for at in range(0, nodes, LANES):
        cols = slice(at, at + LANES)
        v = field[:, cols]
        ham = mass[:, cols] * 0.5 * assembled_columns(banks, at) + pot[:, cols] * v
        piece = first_gain * (ham - shift_center * v)
        first[:, cols] = piece
        table[cols, :] = jnp.concatenate([piece, piece], axis=0).T
    table[nodes:, :] = jnp.zeros((table.shape[0] - nodes, LANES), jnp.float32)
    pack_rows(owner_s, table, packed)


def second_kernel(owner_s, arrived, owned, field, older, mass, pot, second, *banks):
    nodes = field.shape[1]
    collect(owner_s, arrived, owned, banks)
    for at in range(0, nodes, LANES):
        cols = slice(at, at + LANES)
        v = field[:, cols]
        ham = mass[:, cols] * 0.5 * assembled_columns(banks, at) + pot[:, cols] * v
        second[:, cols] = second_gain * (ham - shift_center * v) - memory_gain * older[:, cols]


def on_device(
    orbitals, mass_inv, potential, elem_scale, connectivity, elem_count, owner_node, elem_matrix
):
    orbs, nodes = orbitals.shape
    doms = lax.axis_size("dom")
    subs = lax.axis_size("sub")
    cap = owner_node.shape[3]
    elems = elem_scale.shape[0]
    blocks, half = 3 * subs, cap // 2
    rows_up = (elem_matrix.shape[0] + 127) // 128 * 128
    groups = -(-elem_matrix.shape[0] // 8)
    f32 = jnp.float32
    params = pltpu.CompilerParams(vmem_limit_bytes=VMEM_LIMIT)

    owner = owner_node
    mass = mass_inv.reshape(1, nodes)
    pot = potential.reshape(1, nodes)

    table_shape = jax.ShapeDtypeStruct((nodes + 8, LANES), f32)
    block_shape = jax.ShapeDtypeStruct((blocks, half, LANES), f32)
    field_shape = jax.ShapeDtypeStruct((orbs, nodes), f32)
    owned_shape = jax.ShapeDtypeStruct((nodes, LANES), f32)

    exchange = pl.pallas_call(
        functools.partial(exchange_kernel, doms, subs),
        out_shape=block_shape,
        in_specs=[vmem()],
        out_specs=vmem(),
        scratch_shapes=[
            pltpu.SemaphoreType.DMA((blocks,)),
            pltpu.SemaphoreType.DMA((blocks,)),
        ],
        compiler_params=pltpu.CompilerParams(
            collective_id=0, has_side_effects=True, vmem_limit_bytes=VMEM_LIMIT
        ),
        name="exchange",
    )
    total = nodes + blocks * cap
    element = pl.pallas_call(
        element_kernel,
        out_shape=(owned_shape, block_shape),
        in_specs=[pl.BlockSpec(memory_space=pl.ANY), smem(), smem(), vmem(), vmem(), vmem()],
        out_specs=(vmem(), vmem()),
        scratch_shapes=[
            pltpu.VMEM((total, LANES), f32),
            pltpu.VMEM((rows_up, rows_up), f32),
            pltpu.VMEM((elems // 2, rows_up, LANES), f32),
            pltpu.SemaphoreType.DMA((groups,)),
        ]
        + [pltpu.SMEM((8, elems), jnp.int32)] * groups
        + [pltpu.VMEM((total, LANES), f32)] * BANKS,
        compiler_params=params,
        name="element",
    )
    owner_banks = [pltpu.VMEM((nodes + 8, LANES), f32)] * 4

    table, packed = pl.pallas_call(
        start_kernel,
        out_shape=(table_shape, block_shape),
        in_specs=[smem(), vmem()],
        out_specs=(vmem(), vmem()),
        compiler_params=params,
        name="start",
    )(owner, orbitals)
    owned, partial = element(
        connectivity, elem_scale, elem_count, table, exchange(packed), elem_matrix
    )
    first, table, packed = pl.pallas_call(
        first_kernel,
        out_shape=(field_shape, table_shape, block_shape),
        in_specs=[smem()] + [vmem()] * 5,
        out_specs=(vmem(),) * 3,
        scratch_shapes=owner_banks,
        compiler_params=params,
        name="first",
    )(owner, exchange(partial), owned, orbitals, mass, pot)
    owned, partial = element(
        connectivity, elem_scale, elem_count, table, exchange(packed), elem_matrix
    )
    second = pl.pallas_call(
        second_kernel,
        out_shape=field_shape,
        in_specs=[smem()] + [vmem()] * 6,
        out_specs=vmem(),
        scratch_shapes=owner_banks,
        compiler_params=params,
        name="second",
    )(owner, exchange(partial), owned, first, orbitals, mass, pot)
    return (first, second)


def solution(mesh):
    placed = (
        P(None, ("groups", "dom", "sub")),
        P(("groups", "dom", "sub")),
        P(("groups", "dom", "sub")),
        P(("groups", "dom", "sub")),
        P(None, ("groups", "dom", "sub")),
        P(("groups", "dom", "sub")),
        P(("groups", "dom", "sub"), None, None, None),
        P(),
    )
    return jax.shard_map(
        on_device,
        mesh=mesh,
        in_specs=placed,
        out_specs=(P(None, ("groups", "dom", "sub")), P(None, ("groups", "dom", "sub"))),
        check_vma=False,
    )
```

```python
import functools

import jax
import jax.numpy as jnp
from jax import lax
from jax.experimental import pallas as pl
from jax.experimental.pallas import tpu as pltpu
from jax.sharding import PartitionSpec as P

shift_center = 0.5
first_gain = 0.8
second_gain = 1.2
memory_gain = 0.5

LANES = 128
MESH = pl.DeviceIdType.MESH
VMEM_LIMIT = 58 * 1024 * 1024
BANKS = 8
GROUP = 2


def vmem():
    return pl.BlockSpec(memory_space=pltpu.VMEM)


def smem():
    return pl.BlockSpec(memory_space=pltpu.SMEM)


def low_half(shape):
    return lax.broadcasted_iota(jnp.int32, shape, len(shape) - 1) < LANES // 2


def slot(owner_s, block, k):
    subs = owner_s.shape[2]
    return owner_s[0, block // subs, block % subs, k]


def pack_rows(owner_s, table, packed):
    blocks, half = packed.shape[0], packed.shape[1]
    mask = low_half((1, LANES))

    @pl.loop(0, blocks)
    def _(block):
        for k in range(half):
            low = table[pl.ds(slot(owner_s, block, k), 1), :]
            high = table[pl.ds(slot(owner_s, block, half + k), 1), :]
            packed[block, pl.ds(k, 1), :] = jnp.where(mask, low, high)


def start_kernel(owner_s, field, table, packed):
    nodes = field.shape[1]
    for at in range(0, nodes, LANES):
        piece = field[:, at : at + LANES]
        table[at : at + LANES, :] = jnp.concatenate([piece, piece], axis=0).T
    table[nodes:, :] = jnp.zeros((table.shape[0] - nodes, LANES), jnp.float32)
    pack_rows(owner_s, table, packed)


def exchange_kernel(doms, subs, send, recv, send_sem, recv_sem):
    grp = lax.axis_index("groups")
    dom = lax.axis_index("dom")
    sub = lax.axis_index("sub")
    barrier = pltpu.get_barrier_semaphore()

    def each(action):
        for plane in range(3):
            for peer in range(subs):
                there = dom + plane - 1
                live = jnp.logical_and(there >= 0, there < doms)
                if plane == 1:
                    live = jnp.logical_and(live, sub != peer)

                @pl.when(live)
                def _():
                    action(plane, peer, there)

    def greet(plane, peer, there):
        pl.semaphore_signal(
            barrier, inc=1, device_id=(grp, there, peer), device_id_type=MESH
        )

    def copy(plane, peer, there):
        return pltpu.make_async_remote_copy(
            src_ref=send.at[plane * subs + peer],
            dst_ref=recv.at[(2 - plane) * subs + sub],
            send_sem=send_sem.at[plane * subs + peer],
            recv_sem=recv_sem.at[(2 - plane) * subs + sub],
            device_id=(grp, there, peer),
            device_id_type=MESH,
        )

    def arrival(plane, peer, there):
        return pltpu.make_async_remote_copy(
            src_ref=send.at[plane * subs + peer],
            dst_ref=recv.at[plane * subs + peer],
            send_sem=send_sem.at[plane * subs + peer],
            recv_sem=recv_sem.at[plane * subs + peer],
            device_id=(grp, there, peer),
            device_id_type=MESH,
        )

    each(greet)
    planes = jnp.where(dom > 0, 2, 1) + jnp.where(dom < doms - 1, 1, 0)
    pl.semaphore_wait(barrier, planes * subs - 1)
    each(lambda *where: copy(*where).start())
    each(lambda *where: copy(*where).wait_send())
    each(lambda *where: arrival(*where).wait_recv())


def element_kernel(
    conn, scale_s, count_s, table, ghosts, matrix, owned, partial, full, mat, copied, *scratch
):
    nodes = owned.shape[0]
    blocks, half = ghosts.shape[0], ghosts.shape[1]
    rows = matrix.shape[0]
    pairs = conn.shape[1] // 2
    groups = -(-rows // GROUP)
    conn_s, inputs = scratch[:groups], scratch[groups : groups + 2]
    terms, banks = scratch[groups + 2 : groups + 4], scratch[groups + 4 :]
    mask = low_half((1, LANES))

    copies = []
    for group in range(groups):
        size = min(GROUP, rows - GROUP * group)
        copies.append(
            pltpu.make_async_copy(
                conn.at[pl.ds(GROUP * group, size)],
                conn_s[group].at[pl.ds(0, size)],
                copied.at[group],
            )
        )
        copies[-1].start()

    mat[...] = jnp.zeros_like(mat)
    mat[:rows, : matrix.shape[1]] = matrix[...]
    full[:nodes, :] = table[:nodes, :]
    for block in range(blocks):
        piece = ghosts[block]
        other = pltpu.roll(piece, LANES // 2, axis=1)
        begin = nodes + block * 2 * half
        wide = low_half(piece.shape)
        full[begin : begin + half, :] = jnp.where(wide, piece, other)
        full[begin + half : begin + 2 * half, :] = jnp.where(wide, other, piece)
    zero = jnp.zeros((8, LANES), jnp.float32)

    @pl.loop(0, full.shape[0] // 64)
    def _(n):
        for bank in banks:
            for r in range(0, 64, 8):
                bank[pl.ds(pl.multiple_of(n * 64 + r, 8), 8), :] = zero

    for buffer in inputs + terms:
        buffer[...] = jnp.zeros_like(buffer)
    for copy in copies:
        copy.wait()

    big = mat[...].astype(jnp.bfloat16)
    small = (mat[...] - big.astype(jnp.float32)).astype(jnp.bfloat16)

    def index(j, pair, side):
        return pl.ds(conn_s[j // GROUP][j % GROUP, side * pairs + pair], 1)

    def gather(pair, into):
        for j in range(rows):
            low = full[index(j, pair, 0), :]
            high = full[index(j, pair, 1), :]
            into[j : j + 1, :] = jnp.where(mask, low, high)

    def multiply(pair, source, into):
        low = jnp.where(pair < count_s[0], scale_s[pair], 0.0)
        high = jnp.where(pairs + pair < count_s[0], scale_s[pairs + pair], 0.0)
        piece = source[...] * jnp.where(mask, low, high)
        high = piece.astype(jnp.bfloat16)
        low = (piece - high.astype(jnp.float32)).astype(jnp.bfloat16)
        dot = functools.partial(jnp.dot, preferred_element_type=jnp.float32)
        into[...] = dot(big, high) + (dot(big, low) + dot(small, high))

    def scatter(pair, source):
        for i in range(rows):
            term = source[i : i + 1, :]
            for side in range(2):
                bank = banks[(2 * i + side) % len(banks)]
                at = index(i, pair, side)
                bank[at, :] = bank[at, :] + term

    @pl.loop(0, pairs // 2 + 1)
    def _(n):
        for odd in range(2):
            pair = 2 * n + odd
            before = jnp.maximum(pair - 1, 0)
            scatter(jnp.maximum(pair - 2, 0), terms[odd])
            multiply(jnp.minimum(before, pairs - 1), inputs[1 - odd], terms[1 - odd])
            gather(jnp.minimum(pair, pairs - 1), inputs[odd])

    def summed(begin, size):
        at = pl.ds(begin, size)
        low = sum([bank[at, :] for bank in banks[2::2]], banks[0][at, :])
        high = sum([bank[at, :] for bank in banks[3::2]], banks[1][at, :])
        return jnp.where(low_half((size, LANES)), low, high)

    def doubled(begin, size):
        total = summed(begin, size)
        return total + pltpu.roll(total, LANES // 2, axis=1)

    @pl.loop(0, nodes // 64)
    def _(n):
        begin = pl.multiple_of(n * 64, 64)
        owned[pl.ds(begin, 64), :] = summed(begin, 64)

    @pl.loop(0, blocks)
    def _(block):
        begin = pl.multiple_of(nodes + block * 2 * half, 64)
        partial[block] = jnp.where(
            low_half((half, LANES)), doubled(begin, half), doubled(begin + half, half)
        )


def collect(owner_s, arrived, owned, banks):
    nodes = owned.shape[0]
    blocks, half = arrived.shape[0], arrived.shape[1]
    for bank in banks[:2]:
        bank[:nodes, :] = owned[...]
    for bank in banks[2:]:
        bank[...] = jnp.zeros_like(bank)

    @pl.loop(0, blocks)
    def _(block):
        for k in range(half):
            term = arrived[block, pl.ds(k, 1), :]
            for side in range(2):
                bank = banks[(2 * k + side) % len(banks)]
                at = pl.ds(slot(owner_s, block, side * half + k), 1)
                bank[at, :] = bank[at, :] + term


def assembled_columns(banks, at):
    rows = pl.ds(at, LANES)
    low = sum([bank[rows, :] for bank in banks[2::2]], banks[0][rows, :])
    high = sum([bank[rows, :] for bank in banks[3::2]], banks[1][rows, :])
    both = jnp.where(low_half((LANES, LANES)), low, high).T
    return both[: LANES // 2] + both[LANES // 2 :]


def first_kernel(owner_s, arrived, owned, field, mass, pot, first, table, packed, *banks):
    nodes = field.shape[1]
    collect(owner_s, arrived, owned, banks)
    for at in range(0, nodes, LANES):
        cols = slice(at, at + LANES)
        v = field[:, cols]
        ham = mass[:, cols] * 0.5 * assembled_columns(banks, at) + pot[:, cols] * v
        piece = first_gain * (ham - shift_center * v)
        first[:, cols] = piece
        table[cols, :] = jnp.concatenate([piece, piece], axis=0).T
    table[nodes:, :] = jnp.zeros((table.shape[0] - nodes, LANES), jnp.float32)
    pack_rows(owner_s, table, packed)


def second_kernel(owner_s, arrived, owned, field, older, mass, pot, second, *banks):
    nodes = field.shape[1]
    collect(owner_s, arrived, owned, banks)
    for at in range(0, nodes, LANES):
        cols = slice(at, at + LANES)
        v = field[:, cols]
        ham = mass[:, cols] * 0.5 * assembled_columns(banks, at) + pot[:, cols] * v
        second[:, cols] = second_gain * (ham - shift_center * v) - memory_gain * older[:, cols]


def on_device(
    orbitals, mass_inv, potential, elem_scale, connectivity, elem_count, owner_node, elem_matrix
):
    orbs, nodes = orbitals.shape
    doms = lax.axis_size("dom")
    subs = lax.axis_size("sub")
    cap = owner_node.shape[3]
    elems = elem_scale.shape[0]
    blocks, half = 3 * subs, cap // 2
    rows_up = (elem_matrix.shape[0] + 127) // 128 * 128
    groups = -(-elem_matrix.shape[0] // GROUP)
    f32 = jnp.float32
    params = pltpu.CompilerParams(vmem_limit_bytes=VMEM_LIMIT)

    owner = owner_node
    mass = mass_inv.reshape(1, nodes)
    pot = potential.reshape(1, nodes)

    table_shape = jax.ShapeDtypeStruct((nodes + 8, LANES), f32)
    block_shape = jax.ShapeDtypeStruct((blocks, half, LANES), f32)
    field_shape = jax.ShapeDtypeStruct((orbs, nodes), f32)
    owned_shape = jax.ShapeDtypeStruct((nodes, LANES), f32)

    exchange = pl.pallas_call(
        functools.partial(exchange_kernel, doms, subs),
        out_shape=block_shape,
        in_specs=[vmem()],
        out_specs=vmem(),
        scratch_shapes=[
            pltpu.SemaphoreType.DMA((blocks,)),
            pltpu.SemaphoreType.DMA((blocks,)),
        ],
        compiler_params=pltpu.CompilerParams(
            collective_id=0, has_side_effects=True, vmem_limit_bytes=VMEM_LIMIT
        ),
        name="exchange",
    )
    total = nodes + blocks * cap
    element = pl.pallas_call(
        element_kernel,
        out_shape=(owned_shape, block_shape),
        in_specs=[pl.BlockSpec(memory_space=pl.ANY), smem(), smem(), vmem(), vmem(), vmem()],
        out_specs=(vmem(), vmem()),
        scratch_shapes=[
            pltpu.VMEM((total, LANES), f32),
            pltpu.VMEM((rows_up, rows_up), f32),
            pltpu.SemaphoreType.DMA((groups,)),
        ]
        + [pltpu.SMEM((GROUP, elems), jnp.int32)] * groups
        + [pltpu.VMEM((rows_up, LANES), f32)] * 4
        + [pltpu.VMEM((total, LANES), f32)] * BANKS,
        compiler_params=params,
        name="element",
    )
    owner_banks = [pltpu.VMEM((nodes + 8, LANES), f32)] * 4

    table, packed = pl.pallas_call(
        start_kernel,
        out_shape=(table_shape, block_shape),
        in_specs=[smem(), vmem()],
        out_specs=(vmem(), vmem()),
        compiler_params=params,
        name="start",
    )(owner, orbitals)
    owned, partial = element(
        connectivity, elem_scale, elem_count, table, exchange(packed), elem_matrix
    )
    first, table, packed = pl.pallas_call(
        first_kernel,
        out_shape=(field_shape, table_shape, block_shape),
        in_specs=[smem()] + [vmem()] * 5,
        out_specs=(vmem(),) * 3,
        scratch_shapes=owner_banks,
        compiler_params=params,
        name="first",
    )(owner, exchange(partial), owned, orbitals, mass, pot)
    owned, partial = element(
        connectivity, elem_scale, elem_count, table, exchange(packed), elem_matrix
    )
    second = pl.pallas_call(
        second_kernel,
        out_shape=field_shape,
        in_specs=[smem()] + [vmem()] * 6,
        out_specs=vmem(),
        scratch_shapes=owner_banks,
        compiler_params=params,
        name="second",
    )(owner, exchange(partial), owned, first, orbitals, mass, pot)
    return (first, second)


def solution(mesh):
    placed = (
        P(None, ("groups", "dom", "sub")),
        P(("groups", "dom", "sub")),
        P(("groups", "dom", "sub")),
        P(("groups", "dom", "sub")),
        P(None, ("groups", "dom", "sub")),
        P(("groups", "dom", "sub")),
        P(("groups", "dom", "sub"), None, None, None),
        P(),
    )
    return jax.shard_map(
        on_device,
        mesh=mesh,
        in_specs=placed,
        out_specs=(P(None, ("groups", "dom", "sub")), P(None, ("groups", "dom", "sub"))),
        check_vma=False,
    )
```
